256 devices in a mesh: row: 16 (over z_lo, x), col: 16 (over y, z_hi, core).
Axes of the slice: x: 4, y: 4, z: 8 (z_hi: 2, z_lo: 4; z = z_hi * 4 + z_lo), core: 2. Of those that a mesh axis runs over, the one named last changes fastest.
Arguments:
- tokens: bfloat16 [256, 8192], P('row', 'col'), may hold values from -6 to 6
- gate_weight: bfloat16 [8192, 26624], P('col', 'row'), may hold values from -0.0625 to 0.0625
- up_weight: bfloat16 [8192, 26624], P('col', 'row'), may hold values from -0.0625 to 0.0625
- down_weight: bfloat16 [26624, 8192], P('row', 'col'), may hold values from -0.0390625 to 0.0390625
- out_grad: bfloat16 [256, 8192], P('row', 'col'), may hold values from -6 to 6
Outputs:
- input_grad: bfloat16 [256, 8192], P('row', 'col')
- gate_grad: bfloat16 [8192, 26624], P('col', 'row')
- up_grad: bfloat16 [8192, 26624], P('col', 'row')
- down_grad: bfloat16 [26624, 8192], P('row', 'col')
The draws below stay inside these ranges and needn't reach their ends.
All inputs are finite; a program needn't handle non-finite values.
Results may differ from the reference program's by a relative error of at most 0.005.
Values may be sent and summed in bfloat16 or wider, within the bound.
No kernel may reach another device: no remote copies, remote signals or barrier semaphores. Data moves between devices by JAX's collectives and lax.ppermute only.
A program may use at most 64 MiB of HBM per device.

```python
import jax
import jax.numpy as jnp
from jax import lax

D = 8192
FF = 26624
TOKENS = 256


def levels(own_key, shape, shards, smallest, top_value):
    factor_of = 1.0
    for axis_at, blocks in shards:
        steps = jax.random.uniform(jax.random.fold_in(jax.random.fold_in(own_key, 6), axis_at), (blocks,), jnp.float32, smallest / len(shards), top_value / len(shards))
        factor_of = factor_of * jnp.repeat(jnp.exp(steps), shape[axis_at] // blocks).reshape((-1,) + (1,) * (len(shape) - 1 - axis_at))
    return factor_of


def scatter_about(rng, shape, scale, limit, split=(), dtype=jnp.bfloat16):
    values = jax.random.normal(rng, shape, jnp.float32) * scale
    if len(split) > 0:
        values = levels(rng, shape, split, -0.22, 0.18) * values
    return jnp.clip(values, min=-limit, max=limit).astype(dtype)


def setup_inputs(seed: int = 0) -> dict:
    splits = jax.random.split(jax.random.key(seed), 6)
    tokens = scatter_about(splits[0], (TOKENS, D), 1.0, 6.0, ((0, 16), (1, 16)))
    gate_weight = scatter_about(splits[1], (D, FF), D ** -0.5, 0.0625, ((0, 16), (1, 16)))
    up_weight = scatter_about(splits[2], (D, FF), D ** -0.5, 0.0625, ((0, 16), (1, 16)))
    down_weight = scatter_about(splits[3], (FF, D), FF ** -0.5, 0.0390625, ((0, 16), (1, 16)))
    out_grad = scatter_about(splits[4], (TOKENS, D), 1.0, 6.0, ((0, 16), (1, 16)))
    return {"tokens": tokens, "gate_weight": gate_weight, "up_weight": up_weight, "down_weight": down_weight, "out_grad": out_grad}


def reference(tokens, gate_weight, up_weight, down_weight, out_grad):
    gate = jnp.dot(tokens, gate_weight, preferred_element_type=jnp.float32)
    up = jnp.dot(tokens, up_weight, preferred_element_type=jnp.float32)
    hidden = (jax.nn.silu(gate) * up).astype(jnp.bfloat16)
    hidden_cot = lax.dot_general(out_grad, down_weight, (((1,), (1,)), ((), ())), preferred_element_type=jnp.float32)
    sigma = jax.nn.sigmoid(gate)
    up_cot = (hidden_cot * jax.nn.silu(gate)).astype(jnp.bfloat16)
    gate_cot = (hidden_cot * up * sigma * (1.0 + gate * (1.0 - sigma))).astype(jnp.bfloat16)
    factor = jnp.float32(TOKENS) ** -0.5
    down_grad = (jnp.dot(hidden.T, out_grad, preferred_element_type=jnp.float32) * factor).astype(jnp.bfloat16)
    gate_grad = (jnp.dot(tokens.T, gate_cot, preferred_element_type=jnp.float32) * factor).astype(jnp.bfloat16)
    up_grad = (jnp.dot(tokens.T, up_cot, preferred_element_type=jnp.float32) * factor).astype(jnp.bfloat16)
    input_grad = jnp.dot(gate_cot, gate_weight.T, preferred_element_type=jnp.float32)
    input_grad = input_grad + jnp.dot(up_cot, up_weight.T, preferred_element_type=jnp.float32)
    return input_grad.astype(jnp.bfloat16), gate_grad, up_grad, down_grad
```

```python
import jax
import jax.numpy as jnp
from jax import lax
from jax.sharding import PartitionSpec as P

F32 = jnp.float32
BF16 = jnp.bfloat16


def swapped(axis, mask):
    return lambda a: lax.ppermute(a, axis, [(i, i ^ mask) for i in range(16)])


def on_x(k):
    return swapped("row", k)


def on_z_lo(k):
    return swapped("row", 4 * k)


def on_y(k):
    return swapped("col", 4 * k)


on_z_hi = swapped("col", 2)
on_core = swapped("col", 1)


def xor_blocks(a, place):
    for bit, size in ((4, 32), (2, 16), (1, 8)):
        parts = a.reshape(-1, 2, size, a.shape[1])
        other = jnp.stack((parts[:, 1], parts[:, 0]), axis=1)
        a = jnp.where((place & bit) > 0, other, parts).reshape(a.shape)
    return a


def pointwise(gate, up, hidden_cot):
    sigma = jax.nn.sigmoid(gate)
    silu = gate * sigma
    hidden = (silu * up).astype(BF16)
    up_cot = (hidden_cot * silu).astype(BF16)
    gate_cot = (hidden_cot * up * sigma * (1.0 + gate * (1.0 - sigma))).astype(BF16)
    return jnp.concatenate((hidden, gate_cot, up_cot), axis=1)


def dot(left, right, dims):
    return lax.dot_general(left, right, (dims, ((), ())), preferred_element_type=F32)


def body(tokens, gate_weight, up_weight, down_weight, out_grad):
    width = gate_weight.shape[1]
    depth = tokens.shape[1]
    col = lax.axis_index("col")
    place = (col % 2) * 4 + col // 4

    both = jnp.concatenate((tokens, out_grad), axis=1)
    own = jnp.concatenate([both] + [on_x(k)(both) for k in (1, 2, 3)], axis=0)
    own = xor_blocks(own, place)
    chunks = [own] + [on_z_lo(k)(own) for k in (1, 2, 3)]

    backs, cots = [], []
    for k, chunk in enumerate(chunks):
        token, cot = chunk[:, :depth], chunk[:, depth:]
        part = jnp.concatenate(
            (
                dot(token, gate_weight, ((1,), (0,))),
                dot(token, up_weight, ((1,), (0,))),
                dot(cot, down_weight, ((1,), (1,))),
            ),
            axis=1,
        )
        pair = part[:32] + on_core(part[32:])
        total = pair[:8]
        for q in (1, 2, 3):
            total = total + on_y(q)(pair[8 * q : 8 * q + 8].astype(BF16)).astype(F32)
        total = total + on_z_hi(total.astype(BF16)).astype(F32)
        mine = pointwise(total[:, :width], total[:, width : 2 * width], total[:, 2 * width :])
        half = jnp.concatenate([mine] + [on_y(q)(mine) for q in (1, 2, 3)], axis=0)
        full = jnp.concatenate((half, on_core(half)), axis=0)
        cots.append(full)
        back = dot(full[:, width : 2 * width], gate_weight, ((1,), (1,))) + dot(
            full[:, 2 * width :], up_weight, ((1,), (1,))
        )
        back = xor_blocks(back, place)
        backs.append(back if k == 0 else on_z_lo(k)(back))

    back = backs[0] + backs[1] + backs[2] + backs[3]
    total = back[:16]
    for k in (1, 2, 3):
        total = total + on_x(k)(back[16 * k : 16 * k + 16])
    input_grad = total.astype(BF16)

    panel = jnp.concatenate(chunks, axis=0)
    cots = jnp.concatenate(cots, axis=0)
    factor = F32(panel.shape[0]) ** (-0.5)
    token, cot = panel[:, :depth], panel[:, depth:]
    rows = ((0,), (0,))
    down_grad = (dot(cots[:, :width], cot, rows) * factor).astype(BF16)
    gate_grad = (dot(token, cots[:, width : 2 * width], rows) * factor).astype(BF16)
    up_grad = (dot(token, cots[:, 2 * width :], rows) * factor).astype(BF16)
    return (input_grad, gate_grad, up_grad, down_grad)


def solution(mesh):
    in_specs = (P("row", "col"), P("col", "row"), P("col", "row"), P("row", "col"), P("row", "col"))
    out_specs = (P("row", "col"), P("col", "row"), P("col", "row"), P("row", "col"))
    return jax.shard_map(body, mesh=mesh, in_specs=in_specs, out_specs=out_specs, check_vma=False)
```

```python
import jax
import jax.numpy as jnp
from jax import lax
from jax.sharding import PartitionSpec as P

F32 = jnp.float32
BF16 = jnp.bfloat16


def swapped(axis, mask):
    return lambda a: lax.ppermute(a, axis, [(i, i ^ mask) for i in range(16)])


def on_x(k):
    return swapped("row", k)


def on_z_lo(k):
    return swapped("row", 4 * k)


def on_y(k):
    return swapped("col", 4 * k)


on_z_hi = swapped("col", 2)
on_core = swapped("col", 1)

GROUPS = ((0, 1), (2, 3))


def xor_blocks(a, place):
    for bit, size in ((4, 32), (2, 16), (1, 8)):
        parts = a.reshape(-1, 2, size, a.shape[1])
        other = jnp.stack((parts[:, 1], parts[:, 0]), axis=1)
        a = jnp.where((place & bit) > 0, other, parts).reshape(a.shape)
    return a


def pointwise(gate, up, hidden_cot):
    sigma = jax.nn.sigmoid(gate)
    silu = gate * sigma
    hidden = (silu * up).astype(BF16)
    up_cot = (hidden_cot * silu).astype(BF16)
    gate_cot = (hidden_cot * up * sigma * (1.0 + gate * (1.0 - sigma))).astype(BF16)
    return jnp.concatenate((hidden, gate_cot, up_cot), axis=-1)


def dot(left, right, dims):
    return lax.dot_general(left, right, (dims, ((), ())), preferred_element_type=F32)


def body(tokens, gate_weight, up_weight, down_weight, out_grad):
    width = gate_weight.shape[1]
    depth = tokens.shape[1]
    col = lax.axis_index("col")
    place = (col % 2) * 4 + col // 4

    both = jnp.concatenate((tokens, out_grad), axis=1)
    own = jnp.concatenate([both] + [on_z_lo(k)(both) for k in (1, 2, 3)], axis=0)
    own = xor_blocks(own, place)
    blocks = [own] + [on_x(k)(own) for k in (1, 2, 3)]

    backs, cots, panels = [], [], []
    for group in GROUPS:
        n = len(group)
        chunk = jnp.concatenate([blocks[k] for k in group], axis=0)
        panels.append(chunk)
        token, cot = chunk[:, :depth], chunk[:, depth:]
        part = jnp.concatenate(
            (
                dot(token, gate_weight, ((1,), (0,))),
                dot(token, up_weight, ((1,), (0,))),
                dot(cot, down_weight, ((1,), (1,))),
            ),
            axis=1,
        ).reshape(n, 64, 3 * width)
        pair = part[:, :32] + on_core(part[:, 32:])
        total = pair[:, :8]
        for q in (1, 2, 3):
            total = total + on_y(q)(pair[:, 8 * q : 8 * q + 8].astype(BF16)).astype(F32)
        total = total + on_z_hi(total.astype(BF16)).astype(F32)
        mine = pointwise(total[..., :width], total[..., width : 2 * width], total[..., 2 * width :])
        half = jnp.concatenate([mine] + [on_y(q)(mine) for q in (1, 2, 3)], axis=1)
        full = jnp.concatenate((half, on_core(half)), axis=1).reshape(64 * n, 3 * width)
        cots.append(full)
        back = dot(full[:, width : 2 * width], gate_weight, ((1,), (1,))) + dot(
            full[:, 2 * width :], up_weight, ((1,), (1,))
        )
        for i, k in enumerate(group):
            piece = back[64 * i : 64 * i + 64]
            backs.append(piece if k == 0 else on_x(k)(piece))

    back = xor_blocks(backs[0] + backs[1] + backs[2] + backs[3], place)
    total = back[:16]
    for k in (1, 2, 3):
        total = total + on_z_lo(k)(back[16 * k : 16 * k + 16])
    input_grad = total.astype(BF16)

    panel = jnp.concatenate(panels, axis=0)
    cots = jnp.concatenate(cots, axis=0)
    factor = F32(panel.shape[0]) ** (-0.5)
    token, cot = panel[:, :depth], panel[:, depth:]
    rows = ((0,), (0,))
    down_grad = (dot(cots[:, :width], cot, rows) * factor).astype(BF16)
    gate_grad = (dot(token, cots[:, width : 2 * width], rows) * factor).astype(BF16)
    up_grad = (dot(token, cots[:, 2 * width :], rows) * factor).astype(BF16)
    return (input_grad, gate_grad, up_grad, down_grad)


def solution(mesh):
    in_specs = (P("row", "col"), P("col", "row"), P("col", "row"), P("row", "col"), P("row", "col"))
    out_specs = (P("row", "col"), P("col", "row"), P("col", "row"), P("row", "col"))
    return jax.shard_map(body, mesh=mesh, in_specs=in_specs, out_specs=out_specs, check_vma=False)
```

```python
import jax
import jax.numpy as jnp
from jax import lax
from jax.sharding import PartitionSpec as P

F32 = jnp.float32
BF16 = jnp.bfloat16


def swapped(axis, mask):
    return lambda a: lax.ppermute(a, axis, [(i, i ^ mask) for i in range(16)])


def on_x(k):
    return swapped("row", k)


def on_z_lo(k):
    return swapped("row", 4 * k)


def on_y(k):
    return swapped("col", 4 * k)


on_z_hi = swapped("col", 2)
on_core = swapped("col", 1)

def xor_blocks(a, place):
    for bit, size in ((4, 32), (2, 16), (1, 8)):
        parts = a.reshape(-1, 2, size, a.shape[1])
        other = jnp.stack((parts[:, 1], parts[:, 0]), axis=1)
        a = jnp.where((place & bit) > 0, other, parts).reshape(a.shape)
    return a


def pointwise(gate, up, hidden_cot):
    sigma = jax.nn.sigmoid(gate)
    silu = gate * sigma
    hidden = (silu * up).astype(BF16)
    up_cot = (hidden_cot * silu).astype(BF16)
    gate_cot = (hidden_cot * up * sigma * (1.0 + gate * (1.0 - sigma))).astype(BF16)
    return jnp.concatenate((hidden, gate_cot, up_cot), axis=-1)


def dot(left, right, dims):
    return lax.dot_general(left, right, (dims, ((), ())), preferred_element_type=F32)


def side_by_side(left, right):
    n = left.shape[1]
    zero = jnp.zeros((), left.dtype)
    return lax.pad(left, zero, ((0, 0, 0), (0, n, 0))) + lax.pad(right, zero, ((0, 0, 0), (n, 0, 0)))


def after(value, other):
    return lax.optimization_barrier((value, other))[0]


def body(tokens, gate_weight, up_weight, down_weight, out_grad):
    width = gate_weight.shape[1]
    depth = tokens.shape[1]
    col = lax.axis_index("col")
    place = (col % 2) * 4 + col // 4

    both = side_by_side(tokens, out_grad)
    both = jnp.concatenate((both, on_z_lo(1)(both)), axis=0)
    own = jnp.concatenate((both, on_z_lo(2)(both)), axis=0)
    own = xor_blocks(own, place)
    first = jnp.concatenate((own, on_x(1)(own)), axis=0)
    chunks = (first, on_x(3)(first))

    def partial_sums(chunk):
        token, cot = chunk[:, :depth], chunk[:, depth:]
        part = jnp.concatenate(
            (
                dot(token, gate_weight, ((1,), (0,))),
                dot(token, up_weight, ((1,), (0,))),
                dot(cot, down_weight, ((1,), (1,))),
            ),
            axis=1,
        ).reshape(2, 64, 3 * width)
        return part[:, :32] + on_core(part[:, 32:])

    def traded(keep, sent, mask):
        return keep + on_y(mask)(sent).astype(F32)

    def reduced_on_y(pairs):
        orders = ((1, 3), (3, 1))
        blocks = [[pair[:, 8 * q : 8 * q + 8] for q in range(4)] for pair in pairs]
        sent = [
            jnp.concatenate((b[one], b[one ^ two]), axis=1).astype(BF16)
            for b, (one, two) in zip(blocks, orders)
        ]
        sent = lax.optimization_barrier(sent)
        sums = [
            traded(jnp.concatenate((b[0], b[two]), axis=1), x, one)
            for b, x, (one, two) in zip(blocks, sent, orders)
        ]
        return [traded(t[:, :8], t[:, 8:].astype(BF16), two) for t, (_, two) in zip(sums, orders)]

    def reduced_on_z(total):
        return total + on_z_hi(total.astype(BF16)).astype(F32)

    def gathered_on_y(total):
        mine = pointwise(total[..., :width], total[..., width : 2 * width], total[..., 2 * width :])
        return jnp.concatenate([mine] + [on_y(q)(mine) for q in (1, 2, 3)], axis=1)

    def gathered_on_core(half):
        return jnp.concatenate((half, on_core(half)), axis=1).reshape(128, 3 * width)

    def input_part(full):
        return dot(full[:, width : 2 * width], gate_weight, ((1,), (1,))) + dot(
            full[:, 2 * width :], up_weight, ((1,), (1,))
        )

    totals = reduced_on_y([partial_sums(chunk) for chunk in chunks])
    halves = [gathered_on_y(reduced_on_z(total)) for total in totals]
    full = gathered_on_core(halves[0])
    back = input_part(full)
    fulls = [full, gathered_on_core(after(halves[1], back))]
    back_total = back[:64] + on_x(1)(back[64:])
    back = input_part(fulls[1])
    back_total = back_total + on_x(3)(back[:64]) + on_x(2)(back[64:])
    back_total = xor_blocks(back_total, place)
    total = back_total[:16]
    for k in (1, 2, 3):
        total = total + on_z_lo(k)(back_total[16 * k : 16 * k + 16])
    input_grad = total.astype(BF16)

    panel = jnp.concatenate(chunks, axis=0)
    cots = after(jnp.concatenate(fulls, axis=0), back)
    factor = F32(panel.shape[0]) ** (-0.5)
    token, cot = panel[:, :depth], panel[:, depth:]
    rows = ((0,), (0,))
    down_grad = (dot(cots[:, :width], cot, rows) * factor).astype(BF16)
    gate_grad = (dot(token, cots[:, width : 2 * width], rows) * factor).astype(BF16)
    up_grad = (dot(token, cots[:, 2 * width :], rows) * factor).astype(BF16)
    return (input_grad, gate_grad, up_grad, down_grad)


def solution(mesh):
    in_specs = (P("row", "col"), P("col", "row"), P("col", "row"), P("row", "col"), P("row", "col"))
    out_specs = (P("row", "col"), P("col", "row"), P("col", "row"), P("row", "col"))
    return jax.shard_map(body, mesh=mesh, in_specs=in_specs, out_specs=out_specs, check_vma=False)
```

```python
import jax
import jax.numpy as jnp
from jax import lax
from jax.sharding import PartitionSpec as P

F32 = jnp.float32
BF16 = jnp.bfloat16


def swapped(axis, mask):
    return lambda a: lax.ppermute(a, axis, [(i, i ^ mask) for i in range(16)])


def on_x(k):
    return swapped("row", k)


def on_z_lo(k):
    return swapped("row", 4 * k)


def on_y(k):
    return swapped("col", 4 * k)


on_z_hi = swapped("col", 2)
on_core = swapped("col", 1)

def xor_blocks(a, place):
    for bit, size in ((4, 32), (2, 16), (1, 8)):
        parts = a.reshape(-1, 2, size, a.shape[1])
        other = jnp.stack((parts[:, 1], parts[:, 0]), axis=1)
        a = jnp.where((place & bit) > 0, other, parts).reshape(a.shape)
    return a


def pointwise(gate, up, hidden_cot):
    sigma = jax.nn.sigmoid(gate)
    silu = gate * sigma
    hidden = (silu * up).astype(BF16)
    up_cot = (hidden_cot * silu).astype(BF16)
    gate_cot = (hidden_cot * up * sigma * (1.0 + gate * (1.0 - sigma))).astype(BF16)
    return jnp.concatenate((hidden, gate_cot, up_cot), axis=-1)


def dot(left, right, dims):
    return lax.dot_general(left, right, (dims, ((), ())), preferred_element_type=F32)


def side_by_side(left, right):
    n = left.shape[1]
    zero = jnp.zeros((), left.dtype)
    return lax.pad(left, zero, ((0, 0, 0), (0, n, 0))) + lax.pad(right, zero, ((0, 0, 0), (n, 0, 0)))


def after(value, other):
    return lax.optimization_barrier((value, other))[0]


def body(tokens, gate_weight, up_weight, down_weight, out_grad):
    width = gate_weight.shape[1]
    depth = tokens.shape[1]
    col = lax.axis_index("col")
    place = (col % 2) * 4 + col // 4

    both = side_by_side(tokens, out_grad)
    own = jnp.concatenate([both] + [on_z_lo(k)(both) for k in (1, 2, 3)], axis=0)
    own = xor_blocks(own, place)
    weights = jnp.concatenate((gate_weight, up_weight), axis=1)
    own, weights = lax.optimization_barrier((own, weights))
    chunks = [
        jnp.concatenate((own, on_x(2)(own)), axis=0),
        jnp.concatenate((on_x(1)(own), on_x(3)(own)), axis=0),
    ]

    def partial_sums(chunk):
        token, cot = chunk[:, :depth], chunk[:, depth:]
        part = jnp.concatenate(
            (dot(token, weights, ((1,), (0,))), dot(cot, down_weight, ((1,), (1,)))), axis=1
        ).reshape(2, 64, 3 * width)
        return part[:, :32] + on_core(part[:, 32:])

    def reduced(pair):
        total = pair[:, :8]
        for q in (1, 2, 3):
            total = total + on_y(q)(pair[:, 8 * q : 8 * q + 8].astype(BF16)).astype(F32)
        return total + on_z_hi(total.astype(BF16)).astype(F32)

    def gathered_on_y(total):
        mine = pointwise(total[..., :width], total[..., width : 2 * width], total[..., 2 * width :])
        return jnp.concatenate([mine] + [on_y(q)(mine) for q in (1, 2, 3)], axis=1)

    def gathered_on_core(half):
        return jnp.concatenate((half, on_core(half)), axis=1).reshape(128, 3 * width)

    def input_part(full):
        return dot(full[:, width:], weights, ((1,), (1,)))

    halves = [gathered_on_y(reduced(partial_sums(chunk))) for chunk in chunks]
    full = gathered_on_core(halves[0])
    back = input_part(full)
    fulls = [full, gathered_on_core(after(halves[1], back))]
    back_total = back[:64] + on_x(2)(back[64:])
    back = input_part(fulls[1])
    back_total = back_total + on_x(1)(back[:64]) + on_x(3)(back[64:])
    back_total = xor_blocks(back_total, place)
    total = back_total[:16]
    for k in (1, 2, 3):
        total = total + on_z_lo(k)(back_total[16 * k : 16 * k + 16])
    input_grad = total.astype(BF16)

    panel = jnp.concatenate(chunks, axis=0)
    cots = after(jnp.concatenate(fulls, axis=0), back)
    factor = F32(panel.shape[0]) ** (-0.5)
    token, cot = panel[:, :depth], panel[:, depth:]
    rows = ((0,), (0,))
    down_grad = (dot(cots[:, :width], cot, rows) * factor).astype(BF16)
    gate_grad = (dot(token, cots[:, width : 2 * width], rows) * factor).astype(BF16)
    up_grad = (dot(token, cots[:, 2 * width :], rows) * factor).astype(BF16)
    return (input_grad, gate_grad, up_grad, down_grad)


def solution(mesh):
    in_specs = (P("row", "col"), P("col", "row"), P("col", "row"), P("row", "col"), P("row", "col"))
    out_specs = (P("row", "col"), P("col", "row"), P("col", "row"), P("row", "col"))
    return jax.shard_map(body, mesh=mesh, in_specs=in_specs, out_specs=out_specs, check_vma=False)
```

```python
import jax
import jax.numpy as jnp
from jax import lax
from jax.sharding import PartitionSpec as P

F32 = jnp.float32
BF16 = jnp.bfloat16


def swapped(axis, mask):
    return lambda a: lax.ppermute(a, axis, [(i, i ^ mask) for i in range(16)])


def on_x(k):
    return swapped("row", k)


def on_z_lo(k):
    return swapped("row", 4 * k)


def on_y(one, two):
    pairs = [(i, i ^ (4 * (one, two)[i % 2])) for i in range(16)]
    return lambda a: lax.ppermute(a, "col", pairs)


on_z_hi = swapped("col", 2)
on_core = swapped("col", 1)

def turned(a, size, bits):
    parts = a.reshape(-1, 2, 16 // size, 2, size, a.shape[1])
    other = jnp.stack((parts[:, :, :, 1], parts[:, :, :, 0]), axis=3)
    return jnp.where(jnp.stack(bits).reshape(1, 2, 1, 1, 1, 1), other, parts).reshape(a.shape)


def cores_turned(a, core):
    parts = a.reshape(-1, 2, 32, a.shape[1])
    other = jnp.stack((parts[:, 1], parts[:, 0]), axis=1)
    return jnp.where(core > 0, other, parts).reshape(a.shape)


def pointwise(gate, up, hidden_cot):
    sigma = jax.nn.sigmoid(gate)
    silu = gate * sigma
    hidden = (silu * up).astype(BF16)
    up_cot = (hidden_cot * silu).astype(BF16)
    gate_cot = (hidden_cot * up * sigma * (1.0 + gate * (1.0 - sigma))).astype(BF16)
    return jnp.concatenate((hidden, gate_cot, up_cot), axis=-1)


def dot(left, right, dims):
    return lax.dot_general(left, right, (dims, ((), ())), preferred_element_type=F32)


def side_by_side(left, right):
    n = left.shape[1]
    zero = jnp.zeros((), left.dtype)
    return lax.pad(left, zero, ((0, 0, 0), (0, n, 0))) + lax.pad(right, zero, ((0, 0, 0), (n, 0, 0)))


def after(value, other):
    return lax.optimization_barrier((value, other))[0]


def body(tokens, gate_weight, up_weight, down_weight, out_grad):
    width = gate_weight.shape[1]
    depth = tokens.shape[1]
    col = lax.axis_index("col")
    core, low, high = col % 2, (col // 4) % 2 > 0, col // 8 > 0
    step, turn = (low ^ high, high), (high, low ^ high)

    both = side_by_side(tokens, out_grad)
    own = jnp.concatenate([both] + [on_z_lo(k)(both) for k in (1, 2, 3)], axis=0)
    own = cores_turned(turned(turned(own, 16, step), 8, turn), core)
    weights = jnp.concatenate((gate_weight, up_weight), axis=1)
    own, weights = lax.optimization_barrier((own, weights))
    near = jnp.concatenate((own, on_x(2)(own)), axis=0)
    far = [on_x(1)(own), on_x(3)(own)]

    def partial_sums(chunk):
        token, cot = chunk[:, :depth], chunk[:, depth:]
        return jnp.concatenate(
            (dot(token, weights, ((1,), (0,))), dot(cot, down_weight, ((1,), (1,)))), axis=1
        ).reshape(2, 64, 3 * width)

    def reduced_on_core(part):
        return part[:, :32] + on_core(part[:, 32:])

    def traded(keep, sent, one, two):
        return keep + on_y(one, two)(sent.astype(BF16)).astype(F32)

    def reduced(pair):
        total = traded(pair[:, :16], pair[:, 16:], 1, 3)
        return traded(total[:, :8], total[:, 8:], 3, 1)

    def local(total, other):
        total = total + other.astype(F32)
        return pointwise(total[..., :width], total[..., width : 2 * width], total[..., 2 * width :])

    def gathered_on_y(mine):
        mine = jnp.concatenate((mine, on_y(3, 1)(mine)), axis=1)
        return jnp.concatenate((mine, on_y(1, 3)(mine)), axis=1)

    def joined(half, other):
        return jnp.concatenate((half, other), axis=1).reshape(128, 3 * width)

    def input_part(full):
        return dot(full[:, width:], weights, ((1,), (1,)))

    part = partial_sums(near)
    chunks = [near, jnp.concatenate(after(far, part), axis=0)]
    pairs = [reduced_on_core(part), reduced_on_core(partial_sums(chunks[1]))]
    totals = [reduced(pair) for pair in pairs]
    others = [on_z_hi(total.astype(BF16)) for total in totals]
    first = local(totals[0], others[0])
    second = local(totals[1], after(others[1], first))
    halves = [gathered_on_y(mine) for mine in (first, second)]
    others = [on_core(half) for half in halves]
    fulls = [joined(halves[0], others[0])]
    back = input_part(fulls[0])
    back, sent = back[:64], back[64:]
    fulls.append(joined(halves[1], after(others[1], sent)))
    back_total = back + on_x(2)(sent)
    back = input_part(fulls[1])
    back_total = back_total + on_x(1)(back[:64]) + on_x(3)(back[64:])
    back_total = turned(turned(cores_turned(back_total, core), 16, step), 8, turn)
    total = back_total[:16]
    for k in (1, 2, 3):
        total = total + on_z_lo(k)(back_total[16 * k : 16 * k + 16])
    input_grad = total.astype(BF16)

    panel = jnp.concatenate(chunks, axis=0)
    cots = after(jnp.concatenate(fulls, axis=0), back)
    factor = F32(panel.shape[0]) ** (-0.5)
    token, cot = panel[:, :depth], panel[:, depth:]
    rows = ((0,), (0,))
    down_grad = (dot(cots[:, :width], cot, rows) * factor).astype(BF16)
    gate_grad = (dot(token, cots[:, width : 2 * width], rows) * factor).astype(BF16)
    up_grad = (dot(token, cots[:, 2 * width :], rows) * factor).astype(BF16)
    return (input_grad, gate_grad, up_grad, down_grad)


def solution(mesh):
    in_specs = (P("row", "col"), P("col", "row"), P("col", "row"), P("row", "col"), P("row", "col"))
    out_specs = (P("row", "col"), P("col", "row"), P("col", "row"), P("row", "col"))
    return jax.shard_map(body, mesh=mesh, in_specs=in_specs, out_specs=out_specs, check_vma=False)
```

```python
import jax
import jax.numpy as jnp
from jax import lax
from jax.sharding import PartitionSpec as P

F32 = jnp.float32
BF16 = jnp.bfloat16


def swapped(axis, mask):
    return lambda a: lax.ppermute(a, axis, [(i, i ^ mask) for i in range(16)])


def on_x(k):
    return swapped("row", k)


def on_z_lo(k):
    return swapped("row", 4 * k)


def on_y(k):
    return swapped("col", 4 * k)


on_z_hi = swapped("col", 2)
on_core = swapped("col", 1)

def xor_blocks(a, place):
    for bit, size in ((4, 32), (2, 16), (1, 8)):
        parts = a.reshape(-1, 2, size, a.shape[1])
        other = jnp.stack((parts[:, 1], parts[:, 0]), axis=1)
        a = jnp.where((place & bit) > 0, other, parts).reshape(a.shape)
    return a


def pointwise(gate, up, hidden_cot):
    sigma = jax.nn.sigmoid(gate)
    silu = gate * sigma
    hidden = (silu * up).astype(BF16)
    up_cot = (hidden_cot * silu).astype(BF16)
    gate_cot = (hidden_cot * up * sigma * (1.0 + gate * (1.0 - sigma))).astype(BF16)
    return jnp.concatenate((hidden, gate_cot, up_cot), axis=-1)


def dot(left, right, dims):
    return lax.dot_general(left, right, (dims, ((), ())), preferred_element_type=F32)


def side_by_side(left, right):
    n = left.shape[1]
    zero = jnp.zeros((), left.dtype)
    return lax.pad(left, zero, ((0, 0, 0), (0, n, 0))) + lax.pad(right, zero, ((0, 0, 0), (n, 0, 0)))


def after(value, other):
    return lax.optimization_barrier((value, other))[0]


def body(tokens, gate_weight, up_weight, down_weight, out_grad):
    width = gate_weight.shape[1]
    depth = tokens.shape[1]
    col = lax.axis_index("col")
    place = (col % 2) * 4 + col // 4

    both = side_by_side(tokens, out_grad)
    own = jnp.concatenate([both] + [on_z_lo(k)(both) for k in (1, 2, 3)], axis=0)
    own = xor_blocks(own, place)
    near, far = on_x(2)(own), [on_x(1)(own), on_x(3)(own)]

    def partial_sums(chunk):
        token, cot = chunk[:, :depth], chunk[:, depth:]
        return jnp.concatenate(
            (
                dot(token, gate_weight, ((1,), (0,))),
                dot(token, up_weight, ((1,), (0,))),
                dot(cot, down_weight, ((1,), (1,))),
            ),
            axis=1,
        ).reshape(-1, 64, 3 * width)

    def reduced_on_core(part):
        return part[:, :32] + on_core(part[:, 32:])

    def sent_on_y(pair):
        return [pair[:, 8 * q : 8 * q + 8].astype(BF16) for q in (1, 2, 3)]

    def reduced_on_y(pair, others):
        total = pair[:, :8]
        for other in others:
            total = total + other.astype(F32)
        return total

    def local(total, other):
        total = total + other.astype(F32)
        return pointwise(total[..., :width], total[..., width : 2 * width], total[..., 2 * width :])

    def joined(half, other):
        return jnp.concatenate((half, other), axis=1).reshape(128, 3 * width)

    def input_part(full):
        return dot(full[:, width : 2 * width], gate_weight, ((1,), (1,))) + dot(
            full[:, 2 * width :], up_weight, ((1,), (1,))
        )

    part = partial_sums(own)
    near = after(near, part)
    part = jnp.concatenate((part, partial_sums(near)), axis=0)
    far = jnp.concatenate(after(far, part), axis=0)
    pairs = [reduced_on_core(part), reduced_on_core(partial_sums(far))]
    sent = [sent_on_y(pair) for pair in pairs]
    others = [[on_y(q)(blocks[q - 1]) for q in (1, 2, 3)] for blocks in sent]
    totals = [
        reduced_on_y(pairs[0], after(others[0], sent[1])),
        reduced_on_y(pairs[1], others[1]),
    ]
    sent = [total.astype(BF16) for total in totals]
    others = [on_z_hi(total) for total in sent]
    first = local(totals[0], after(others[0], sent[1]))
    second = local(totals[1], others[1])
    others = [[on_y(q)(mine) for q in (1, 2, 3)] for mine in (first, second)]
    halves = [
        jnp.concatenate([first] + after(others[0], second), axis=1),
        jnp.concatenate([second] + others[1], axis=1),
    ]
    others = [on_core(half) for half in halves]
    fulls = [joined(halves[0], others[0])]
    back = input_part(fulls[0])
    back, sent = back[:64], back[64:]
    fulls.append(joined(halves[1], after(others[1], sent)))
    back_total = back + on_x(2)(sent)
    back = input_part(fulls[1])
    back_total = back_total + on_x(1)(back[:64]) + on_x(3)(back[64:])
    back_total = xor_blocks(back_total, place)
    total = back_total[:16]
    for k in (1, 2, 3):
        total = total + on_z_lo(k)(back_total[16 * k : 16 * k + 16])
    input_grad = total.astype(BF16)

    panel = jnp.concatenate((own, near, far), axis=0)
    cots = after(jnp.concatenate(fulls, axis=0), back)
    factor = F32(panel.shape[0]) ** (-0.5)
    token, cot = panel[:, :depth], panel[:, depth:]
    rows = ((0,), (0,))
    down_grad = (dot(cots[:, :width], cot, rows) * factor).astype(BF16)
    gate_grad = (dot(token, cots[:, width : 2 * width], rows) * factor).astype(BF16)
    up_grad = (dot(token, cots[:, 2 * width :], rows) * factor).astype(BF16)
    return (input_grad, gate_grad, up_grad, down_grad)


def solution(mesh):
    in_specs = (P("row", "col"), P("col", "row"), P("col", "row"), P("row", "col"), P("row", "col"))
    out_specs = (P("row", "col"), P("col", "row"), P("col", "row"), P("row", "col"))
    return jax.shard_map(body, mesh=mesh, in_specs=in_specs, out_specs=out_specs, check_vma=False)
```

```python
import jax
import jax.numpy as jnp
from jax import lax
from jax.sharding import PartitionSpec as P

F32 = jnp.float32
BF16 = jnp.bfloat16


def swapped(axis, mask):
    return lambda a: lax.ppermute(a, axis, [(i, i ^ mask) for i in range(16)])


def on_x(k):
    return swapped("row", k)


def on_z_lo(k):
    return swapped("row", 4 * k)


def on_y(k):
    return swapped("col", 4 * k)


on_z_hi = swapped("col", 2)
on_core = swapped("col", 1)

def xor_blocks(a, place):
    for bit, size in ((4, 32), (2, 16), (1, 8)):
        parts = a.reshape(-1, 2, size, a.shape[1])
        other = jnp.stack((parts[:, 1], parts[:, 0]), axis=1)
        a = jnp.where((place & bit) > 0, other, parts).reshape(a.shape)
    return a


def pointwise(gate, up, hidden_cot):
    sigma = jax.nn.sigmoid(gate)
    silu = gate * sigma
    hidden = (silu * up).astype(BF16)
    up_cot = (hidden_cot * silu).astype(BF16)
    gate_cot = (hidden_cot * up * sigma * (1.0 + gate * (1.0 - sigma))).astype(BF16)
    return jnp.concatenate((hidden, gate_cot, up_cot), axis=-1)


def dot(left, right, dims):
    return lax.dot_general(left, right, (dims, ((), ())), preferred_element_type=F32)


def side_by_side(left, right):
    n = left.shape[1]
    zero = jnp.zeros((), left.dtype)
    return lax.pad(left, zero, ((0, 0, 0), (0, n, 0))) + lax.pad(right, zero, ((0, 0, 0), (n, 0, 0)))


def after(value, other):
    return lax.optimization_barrier((value, other))[0]


def body(tokens, gate_weight, up_weight, down_weight, out_grad):
    width = gate_weight.shape[1]
    depth = tokens.shape[1]
    col = lax.axis_index("col")
    place = (col % 2) * 4 + col // 4

    both = side_by_side(tokens, out_grad)
    own = jnp.concatenate([both] + [on_z_lo(k)(both) for k in (3, 2, 1)], axis=0)
    own = xor_blocks(own, place)
    near, far = on_x(2)(own), [on_x(1)(own), on_x(3)(own)]

    def partial_sums(chunk):
        token, cot = chunk[:, :depth], chunk[:, depth:]
        return jnp.concatenate(
            (
                dot(token, gate_weight, ((1,), (0,))),
                dot(token, up_weight, ((1,), (0,))),
                dot(cot, down_weight, ((1,), (1,))),
            ),
            axis=1,
        ).reshape(-1, 64, 3 * width)

    def reduced_on_core(part):
        return part[:, :32] + on_core(part[:, 32:])

    def sent_on_y(pair):
        return [pair[:, 8 * q : 8 * q + 8].astype(BF16) for q in (3, 2, 1)]

    def reduced_on_y(pair, others):
        total = pair[:, :8]
        for other in others:
            total = total + other.astype(F32)
        return total

    def local(total, other):
        total = total + other.astype(F32)
        return pointwise(total[..., :width], total[..., width : 2 * width], total[..., 2 * width :])

    def joined(half, other):
        return jnp.concatenate((half, other), axis=1).reshape(128, 3 * width)

    def input_part(full):
        return dot(full[:, width : 2 * width], gate_weight, ((1,), (1,))) + dot(
            full[:, 2 * width :], up_weight, ((1,), (1,))
        )

    part = partial_sums(own)
    near = after(near, part)
    part = jnp.concatenate((part, partial_sums(near)), axis=0)
    far = jnp.concatenate(after(far, part), axis=0)
    pairs = [reduced_on_core(part), reduced_on_core(partial_sums(far))]
    sent = [sent_on_y(pair) for pair in pairs]
    others = [[on_y(q)(block) for q, block in zip((3, 2, 1), blocks)] for blocks in sent]
    totals = [
        reduced_on_y(pairs[0], after(others[0], sent[1])),
        reduced_on_y(pairs[1], others[1]),
    ]
    sent = [total.astype(BF16) for total in totals]
    others = [on_z_hi(total) for total in sent]
    first = local(totals[0], after(others[0], sent[1]))
    second = local(totals[1], others[1])
    others = [
        after([on_y(q)(first) for q in (1, 2, 3)], second),
        after([on_y(q)(second) for q in (3, 2, 1)], first)[::-1],
    ]
    halves = [jnp.concatenate([a] + b, axis=1) for a, b in zip((first, second), others)]
    others = [on_core(half) for half in halves]
    fulls = [joined(halves[0], others[0])]
    back = input_part(fulls[0])
    back, sent = back[:64], back[64:]
    fulls.append(joined(halves[1], after(others[1], sent)))
    back_total = back + on_x(2)(sent)
    back = input_part(fulls[1])
    back_total = back_total + on_x(3)(back[64:]) + on_x(1)(back[:64])
    back_total = xor_blocks(back_total, place)
    total = back_total[:16]
    for i, k in enumerate((3, 2, 1)):
        total = total + on_z_lo(k)(back_total[16 * i + 16 : 16 * i + 32])
    input_grad = total.astype(BF16)

    panel = jnp.concatenate((own, near, far), axis=0)
    cots = after(jnp.concatenate(fulls, axis=0), back)
    factor = F32(panel.shape[0]) ** (-0.5)
    token, cot = panel[:, :depth], panel[:, depth:]
    rows = ((0,), (0,))
    down_grad = (dot(cots[:, :width], cot, rows) * factor).astype(BF16)
    gate_grad = (dot(token, cots[:, width : 2 * width], rows) * factor).astype(BF16)
    up_grad = (dot(token, cots[:, 2 * width :], rows) * factor).astype(BF16)
    return (input_grad, gate_grad, up_grad, down_grad)


def solution(mesh):
    in_specs = (P("row", "col"), P("col", "row"), P("col", "row"), P("row", "col"), P("row", "col"))
    out_specs = (P("row", "col"), P("col", "row"), P("col", "row"), P("row", "col"))
    return jax.shard_map(body, mesh=mesh, in_specs=in_specs, out_specs=out_specs, check_vma=False)
```

```python
import jax
import jax.numpy as jnp
from jax import lax
from jax.sharding import PartitionSpec as P

F32 = jnp.float32
BF16 = jnp.bfloat16


def swapped(axis, mask):
    return lambda a: lax.ppermute(a, axis, [(i, i ^ mask) for i in range(16)])


def on_x(k):
    return swapped("row", k)


def on_z_lo(k):
    return swapped("row", 4 * k)


def on_y(k):
    return swapped("col", 4 * k)


on_z_hi = swapped("col", 2)
on_core = swapped("col", 1)

def xor_blocks(a, place):
    for bit, size in ((4, 32), (2, 16), (1, 8)):
        parts = a.reshape(-1, 2, size, a.shape[1])
        other = jnp.stack((parts[:, 1], parts[:, 0]), axis=1)
        a = jnp.where((place & bit) > 0, other, parts).reshape(a.shape)
    return a


def pointwise(gate, up, hidden_cot):
    sigma = jax.nn.sigmoid(gate)
    silu = gate * sigma
    hidden = (silu * up).astype(BF16)
    up_cot = (hidden_cot * silu).astype(BF16)
    gate_cot = (hidden_cot * up * sigma * (1.0 + gate * (1.0 - sigma))).astype(BF16)
    return jnp.concatenate((hidden, gate_cot, up_cot), axis=-1)


def dot(left, right, dims):
    return lax.dot_general(left, right, (dims, ((), ())), preferred_element_type=F32)


def side_by_side(left, right):
    n = left.shape[1]
    zero = jnp.zeros((), left.dtype)
    return lax.pad(left, zero, ((0, 0, 0), (0, n, 0))) + lax.pad(right, zero, ((0, 0, 0), (n, 0, 0)))


def after(value, other):
    return lax.optimization_barrier((value, other))[0]


def body(tokens, gate_weight, up_weight, down_weight, out_grad):
    width = gate_weight.shape[1]
    depth = tokens.shape[1]
    col = lax.axis_index("col")
    place = (col % 2) * 4 + col // 4

    both = side_by_side(tokens, out_grad)
    own = jnp.concatenate([both] + [on_z_lo(k)(both) for k in (3, 2, 1)], axis=0)
    own = xor_blocks(own, place)
    near, far = on_x(2)(own), [on_x(1)(own), on_x(3)(own)]

    def partial_sums(chunk):
        token, cot = chunk[:, :depth], chunk[:, depth:]
        return jnp.concatenate(
            (
                dot(token, gate_weight, ((1,), (0,))),
                dot(token, up_weight, ((1,), (0,))),
                dot(cot, down_weight, ((1,), (1,))),
            ),
            axis=1,
        ).reshape(-1, 64, 3 * width)

    def reduced_on_core(part):
        return part[:, :32] + on_core(part[:, 32:])

    def sent_on_y(pair):
        return [pair[:, 8 * q : 8 * q + 8].astype(BF16) for q in (3, 2, 1)]

    def reduced_on_y(pair, others):
        total = pair[:, :8]
        for other in others:
            total = total + other.astype(F32)
        return total

    def local(total, other):
        total = total + other.astype(F32)
        return pointwise(total[..., :width], total[..., width : 2 * width], total[..., 2 * width :])

    def joined(half, other):
        return jnp.concatenate((half, other), axis=1).reshape(128, 3 * width)

    def input_part(full):
        return dot(full[:, width : 2 * width], gate_weight, ((1,), (1,))) + dot(
            full[:, 2 * width :], up_weight, ((1,), (1,))
        )

    part = partial_sums(own)
    near = after(near, part)
    part = jnp.concatenate((part, partial_sums(near)), axis=0)
    far = jnp.concatenate(after(far, part), axis=0)
    pairs = [reduced_on_core(part), reduced_on_core(partial_sums(far))]
    sent = [sent_on_y(pair) for pair in pairs]
    others = [[on_y(q)(block) for q, block in zip((3, 2, 1), blocks)] for blocks in sent]
    totals = [
        reduced_on_y(pairs[0], after(others[0], sent[1])),
        reduced_on_y(pairs[1], others[1]),
    ]
    sent = [total.astype(BF16) for total in totals]
    others = [on_z_hi(total) for total in sent]
    first = local(totals[0], after(others[0], sent[1]))
    second = local(totals[1], others[1])
    others = [on_y(q)(first) for q in (1, 2, 3)], [on_y(q)(second) for q in (3, 2, 1)]
    half = jnp.concatenate([first] + after(others[0], second), axis=1)
    fulls = [joined(half, on_core(half))]
    back = input_part(fulls[0])
    back, sent = back[:64], back[64:]
    half = jnp.concatenate([second] + after(others[1], sent)[::-1], axis=1)
    fulls.append(joined(half, on_core(half)))
    back_total = back + on_x(2)(sent)
    back = input_part(fulls[1])
    back_total = back_total + on_x(3)(back[64:]) + on_x(1)(back[:64])
    back_total = xor_blocks(back_total, place)
    total = back_total[:16]
    for i, k in enumerate((3, 2, 1)):
        total = total + on_z_lo(k)(back_total[16 * i + 16 : 16 * i + 32])
    input_grad = total.astype(BF16)

    panel = jnp.concatenate((own, near, far), axis=0)
    cots = after(jnp.concatenate(fulls, axis=0), back)
    factor = F32(panel.shape[0]) ** (-0.5)
    token, cot = panel[:, :depth], panel[:, depth:]
    rows = ((0,), (0,))
    down_grad = (dot(cots[:, :width], cot, rows) * factor).astype(BF16)
    gate_grad = (dot(token, cots[:, width : 2 * width], rows) * factor).astype(BF16)
    up_grad = (dot(token, cots[:, 2 * width :], rows) * factor).astype(BF16)
    return (input_grad, gate_grad, up_grad, down_grad)


def solution(mesh):
    in_specs = (P("row", "col"), P("col", "row"), P("col", "row"), P("row", "col"), P("row", "col"))
    out_specs = (P("row", "col"), P("col", "row"), P("col", "row"), P("row", "col"))
    return jax.shard_map(body, mesh=mesh, in_specs=in_specs, out_specs=out_specs, check_vma=False)
```

```python
import jax
import jax.numpy as jnp
from jax import lax
from jax.sharding import PartitionSpec as P

F32 = jnp.float32
BF16 = jnp.bfloat16


def swapped(axis, mask):
    return lambda a: lax.ppermute(a, axis, [(i, i ^ mask) for i in range(16)])


def on_x(k):
    return swapped("row", k)


def on_z_lo(k):
    return swapped("row", 4 * k)


def on_y(k):
    return swapped("col", 4 * k)


on_z_hi = swapped("col", 2)
on_core = swapped("col", 1)

def xor_blocks(a, place):
    for bit, size in ((4, 32), (2, 16), (1, 8)):
        parts = a.reshape(-1, 2, size, a.shape[1])
        other = jnp.stack((parts[:, 1], parts[:, 0]), axis=1)
        a = jnp.where((place & bit) > 0, other, parts).reshape(a.shape)
    return a


def pointwise(gate, up, hidden_cot):
    sigma = jax.nn.sigmoid(gate)
    silu = gate * sigma
    hidden = (silu * up).astype(BF16)
    up_cot = (hidden_cot * silu).astype(BF16)
    gate_cot = (hidden_cot * up * sigma * (1.0 + gate * (1.0 - sigma))).astype(BF16)
    return jnp.concatenate((hidden, gate_cot, up_cot), axis=-1)


def dot(left, right, dims):
    return lax.dot_general(left, right, (dims, ((), ())), preferred_element_type=F32)


def side_by_side(left, right):
    n = left.shape[1]
    zero = jnp.zeros((), left.dtype)
    return lax.pad(left, zero, ((0, 0, 0), (0, n, 0))) + lax.pad(right, zero, ((0, 0, 0), (n, 0, 0)))


def after(value, other):
    return lax.optimization_barrier((value, other))[0]


def body(tokens, gate_weight, up_weight, down_weight, out_grad):
    width = gate_weight.shape[1]
    depth = tokens.shape[1]
    col = lax.axis_index("col")
    place = (col % 2) * 4 + col // 4

    both = side_by_side(tokens, out_grad)
    own = jnp.concatenate([both] + [on_z_lo(k)(both) for k in (1, 2, 3)], axis=0)
    own = xor_blocks(own, place)
    near, far = on_x(2)(own), [on_x(1)(own), on_x(3)(own)]

    def partial_sums(chunk):
        token, cot = chunk[:, :depth], chunk[:, depth:]
        return jnp.concatenate(
            (
                dot(token, gate_weight, ((1,), (0,))),
                dot(token, up_weight, ((1,), (0,))),
                dot(cot, down_weight, ((1,), (1,))),
            ),
            axis=1,
        ).reshape(-1, 64, 3 * width)

    def reduced_on_core(part):
        return part[:, :32] + on_core(part[:, 32:])

    def sent_on_y(pair, order):
        return [pair[:, 8 * q : 8 * q + 8].astype(BF16) for q in order]

    def reduced_on_y(pair, others):
        total = pair[:, :8]
        for other in others:
            total = total + other.astype(F32)
        return total

    def local(total, other):
        total = total + other.astype(F32)
        return pointwise(total[..., :width], total[..., width : 2 * width], total[..., 2 * width :])

    def joined(half, other):
        return jnp.concatenate((half, other), axis=1).reshape(128, 3 * width)

    def input_part(full):
        return dot(full[:, width : 2 * width], gate_weight, ((1,), (1,))) + dot(
            full[:, 2 * width :], up_weight, ((1,), (1,))
        )

    part = partial_sums(own)
    pair = reduced_on_core(part)
    rest = jnp.concatenate(after(far + [near], part), axis=0)
    part = partial_sums(rest)
    pairs = [
        jnp.concatenate((pair, reduced_on_core(part[2:])), axis=0),
        reduced_on_core(part[:2]),
    ]
    orders = ((1, 2, 3), (3, 1, 2))
    sent = [sent_on_y(pair, order) for pair, order in zip(pairs, orders)]
    others = [
        [on_y(q)(block) for q, block in zip(order, blocks)] for order, blocks in zip(orders, sent)
    ]
    totals = [
        reduced_on_y(pairs[0], after(others[0], sent[1])),
        reduced_on_y(pairs[1], others[1]),
    ]
    sent = [total.astype(BF16) for total in totals]
    others = [on_z_hi(total) for total in sent]
    first = local(totals[0], after(others[0], sent[1]))
    second = local(totals[1], others[1])
    others = [
        after([on_y(q)(first) for q in (3, 2, 1)], second)[::-1],
        after([on_y(q)(second) for q in (1, 2, 3)], first),
    ]
    halves = [jnp.concatenate([a] + b, axis=1) for a, b in zip((first, second), others)]
    others = [on_core(half) for half in halves]
    fulls = [joined(halves[0], others[0])]
    back = input_part(fulls[0])
    back, sent = back[:64], back[64:]
    fulls.append(joined(halves[1], after(others[1], sent)))
    back_total = back + on_x(2)(sent)
    back = input_part(fulls[1])
    back_total = back_total + on_x(3)(back[64:]) + on_x(1)(back[:64])
    back_total = xor_blocks(back_total, place)
    total = back_total[:16]
    for k in (3, 1, 2):
        total = total + on_z_lo(k)(back_total[16 * k : 16 * k + 16])
    input_grad = total.astype(BF16)

    panel = jnp.concatenate((own, near, rest[:128]), axis=0)
    cots = after(jnp.concatenate(fulls, axis=0), back)
    factor = F32(panel.shape[0]) ** (-0.5)
    token, cot = panel[:, :depth], panel[:, depth:]
    rows = ((0,), (0,))
    down_grad = (dot(cots[:, :width], cot, rows) * factor).astype(BF16)
    gate_grad = (dot(token, cots[:, width : 2 * width], rows) * factor).astype(BF16)
    up_grad = (dot(token, cots[:, 2 * width :], rows) * factor).astype(BF16)
    return (input_grad, gate_grad, up_grad, down_grad)


def solution(mesh):
    in_specs = (P("row", "col"), P("col", "row"), P("col", "row"), P("row", "col"), P("row", "col"))
    out_specs = (P("row", "col"), P("col", "row"), P("col", "row"), P("row", "col"))
    return jax.shard_map(body, mesh=mesh, in_specs=in_specs, out_specs=out_specs, check_vma=False)
```

```python
import jax
import jax.numpy as jnp
from jax import lax
from jax.sharding import PartitionSpec as P

F32 = jnp.float32
BF16 = jnp.bfloat16


def swapped(axis, mask):
    return lambda a: lax.ppermute(a, axis, [(i, i ^ mask) for i in range(16)])


def on_x(k):
    return swapped("row", k)


def on_z_lo(k):
    return swapped("row", 4 * k)


def on_y(k):
    return swapped("col", 4 * k)


on_z_hi = swapped("col", 2)
on_core = swapped("col", 1)

def xor_blocks(a, place):
    for bit, size in ((4, 32), (2, 16), (1, 8)):
        parts = a.reshape(-1, 2, size, a.shape[1])
        other = jnp.stack((parts[:, 1], parts[:, 0]), axis=1)
        a = jnp.where((place & bit) > 0, other, parts).reshape(a.shape)
    return a


def pointwise(gate, up, hidden_cot):
    sigma = jax.nn.sigmoid(gate)
    silu = gate * sigma
    hidden = (silu * up).astype(BF16)
    up_cot = (hidden_cot * silu).astype(BF16)
    gate_cot = (hidden_cot * up * sigma * (1.0 + gate * (1.0 - sigma))).astype(BF16)
    return jnp.concatenate((hidden, gate_cot, up_cot), axis=-1)


def dot(left, right, dims):
    return lax.dot_general(left, right, (dims, ((), ())), preferred_element_type=F32)


def side_by_side(left, right):
    n = left.shape[1]
    zero = jnp.zeros((), left.dtype)
    return lax.pad(left, zero, ((0, 0, 0), (0, n, 0))) + lax.pad(right, zero, ((0, 0, 0), (n, 0, 0)))


def after(value, other):
    return lax.optimization_barrier((value, other))[0]


def body(tokens, gate_weight, up_weight, down_weight, out_grad):
    width = gate_weight.shape[1]
    depth = tokens.shape[1]
    col = lax.axis_index("col")
    place = (col % 2) * 4 + col // 4

    both = side_by_side(tokens, out_grad)
    own = jnp.concatenate([both] + [on_z_lo(k)(both) for k in (3, 2, 1)], axis=0)
    own = xor_blocks(own, place)
    near, far = on_x(2)(own), [on_x(1)(own), on_x(3)(own)]

    def partial_sums(chunk):
        token, cot = chunk[:, :depth], chunk[:, depth:]
        return jnp.concatenate(
            (
                dot(token, gate_weight, ((1,), (0,))),
                dot(token, up_weight, ((1,), (0,))),
                dot(cot, down_weight, ((1,), (1,))),
            ),
            axis=1,
        ).reshape(-1, 64, 3 * width)

    def reduced_on_core(part):
        return part[:, :32] + on_core(part[:, 32:])

    def sent_on_y(pair):
        return [pair[:, 8 * q : 8 * q + 8].astype(BF16) for q in (3, 2, 1)]

    def reduced_on_y(pair, others):
        total = pair[:, :8]
        for other in others:
            total = total + other.astype(F32)
        return total

    def local(total, other):
        total = total + other.astype(F32)
        return pointwise(total[..., :width], total[..., width : 2 * width], total[..., 2 * width :])

    def joined(half, other):
        return jnp.concatenate((half, other), axis=1).reshape(128, 3 * width)

    def input_part(full):
        return dot(full[:, width : 2 * width], gate_weight, ((1,), (1,))) + dot(
            full[:, 2 * width :], up_weight, ((1,), (1,))
        )

    part = partial_sums(own)
    near = after(near, part)
    part = jnp.concatenate((part, partial_sums(near)), axis=0)
    far = jnp.concatenate(after(far, part), axis=0)
    pairs = [reduced_on_core(part), reduced_on_core(partial_sums(far))]
    sent = [sent_on_y(pair) for pair in pairs]
    others = [[on_y(q)(block) for q, block in zip((3, 2, 1), blocks)] for blocks in sent]
    totals = [
        reduced_on_y(pairs[0], after(others[0], sent[1])),
        reduced_on_y(pairs[1], others[1]),
    ]
    sent = [total.astype(BF16) for total in totals]
    others = [jnp.stack([on_z_hi(total[i]) for i in range(2)]) for total in sent]
    first = local(totals[0], after(others[0], sent[1]))
    second = local(totals[1], others[1])
    others = [
        after([on_y(q)(first) for q in (1, 2, 3)], second),
        after([on_y(q)(second) for q in (3, 2, 1)], first)[::-1],
    ]
    halves = [jnp.concatenate([a] + b, axis=1) for a, b in zip((first, second), others)]
    others = [on_core(half) for half in halves]
    fulls = [joined(halves[0], others[0])]
    back = input_part(fulls[0])
    back, sent = back[:64], back[64:]
    fulls.append(joined(halves[1], after(others[1], sent)))
    back_total = back + on_x(2)(sent)
    back = input_part(fulls[1])
    back_total = back_total + on_x(3)(back[64:]) + on_x(1)(back[:64])
    back_total = xor_blocks(back_total, place)
    total = back_total[:16]
    for i, k in enumerate((3, 2, 1)):
        total = total + on_z_lo(k)(back_total[16 * i + 16 : 16 * i + 32])
    input_grad = total.astype(BF16)

    panel = jnp.concatenate((own, near, far), axis=0)
    cots = after(jnp.concatenate(fulls, axis=0), back)
    factor = F32(panel.shape[0]) ** (-0.5)
    token, cot = panel[:, :depth], panel[:, depth:]
    rows = ((0,), (0,))
    down_grad = (dot(cots[:, :width], cot, rows) * factor).astype(BF16)
    gate_grad = (dot(token, cots[:, width : 2 * width], rows) * factor).astype(BF16)
    up_grad = (dot(token, cots[:, 2 * width :], rows) * factor).astype(BF16)
    return (input_grad, gate_grad, up_grad, down_grad)


def solution(mesh):
    in_specs = (P("row", "col"), P("col", "row"), P("col", "row"), P("row", "col"), P("row", "col"))
    out_specs = (P("row", "col"), P("col", "row"), P("col", "row"), P("row", "col"))
    return jax.shard_map(body, mesh=mesh, in_specs=in_specs, out_specs=out_specs, check_vma=False)
```

```python
import jax
import jax.numpy as jnp
from jax import lax
from jax.sharding import PartitionSpec as P

F32 = jnp.float32
BF16 = jnp.bfloat16


def swapped(axis, mask):
    return lambda a: lax.ppermute(a, axis, [(i, i ^ mask) for i in range(16)])


def on_x(k):
    return swapped("row", k)


def on_z_lo(k):
    return swapped("row", 4 * k)


def on_y(k):
    return swapped("col", 4 * k)


on_z_hi = swapped("col", 2)
on_core = swapped("col", 1)

def xor_blocks(a, place):
    for bit, size in ((4, 32), (2, 16), (1, 8)):
        parts = a.reshape(-1, 2, size, a.shape[1])
        other = jnp.stack((parts[:, 1], parts[:, 0]), axis=1)
        a = jnp.where((place & bit) > 0, other, parts).reshape(a.shape)
    return a


def pointwise(gate, up, hidden_cot):
    sigma = jax.nn.sigmoid(gate)
    silu = gate * sigma
    hidden = (silu * up).astype(BF16)
    up_cot = (hidden_cot * silu).astype(BF16)
    gate_cot = (hidden_cot * up * sigma * (1.0 + gate * (1.0 - sigma))).astype(BF16)
    return jnp.concatenate((hidden, gate_cot, up_cot), axis=-1)


def dot(left, right, dims):
    return lax.dot_general(left, right, (dims, ((), ())), preferred_element_type=F32)


def side_by_side(left, right):
    n = left.shape[1]
    zero = jnp.zeros((), left.dtype)
    return lax.pad(left, zero, ((0, 0, 0), (0, n, 0))) + lax.pad(right, zero, ((0, 0, 0), (n, 0, 0)))


def after(value, other):
    return lax.optimization_barrier((value, other))[0]


def body(tokens, gate_weight, up_weight, down_weight, out_grad):
    width = gate_weight.shape[1]
    depth = tokens.shape[1]
    col = lax.axis_index("col")
    place = (col % 2) * 4 + col // 4

    both = side_by_side(tokens, out_grad)
    own = jnp.concatenate([both] + [on_z_lo(k)(both) for k in (1, 2, 3)], axis=0)
    own = xor_blocks(own, place)
    near, far = on_x(2)(own), [on_x(1)(own), on_x(3)(own)]

    def partial_sums(chunk):
        token, cot = chunk[:, :depth], chunk[:, depth:]
        return jnp.concatenate(
            (
                dot(token, gate_weight, ((1,), (0,))),
                dot(token, up_weight, ((1,), (0,))),
                dot(cot, down_weight, ((1,), (1,))),
            ),
            axis=1,
        ).reshape(-1, 64, 3 * width)

    def reduced_on_core(part):
        return part[:, :32] + on_core(part[:, 32:])

    def sent_on_y(pair, order):
        return [pair[:, 8 * q : 8 * q + 8].astype(BF16) for q in order]

    def reduced_on_y(pair, others):
        total = pair[:, :8]
        for other in others:
            total = total + other.astype(F32)
        return total

    def local(total, other):
        total = total + other.astype(F32)
        return pointwise(total[..., :width], total[..., width : 2 * width], total[..., 2 * width :])

    def joined(half, other):
        return jnp.concatenate((half, other), axis=1).reshape(128, 3 * width)

    def input_part(full):
        return dot(full[:, width : 2 * width], gate_weight, ((1,), (1,))) + dot(
            full[:, 2 * width :], up_weight, ((1,), (1,))
        )

    part = partial_sums(own)
    pair = reduced_on_core(part)
    rest = jnp.concatenate(after([near] + far, part), axis=0)
    part = partial_sums(rest)
    pairs = [
        jnp.concatenate((pair, reduced_on_core(part[:1])), axis=0),
        reduced_on_core(part[1:]),
    ]
    orders = ((3, 2, 1), (1, 2, 3))
    sent = [sent_on_y(pair, order) for pair, order in zip(pairs, orders)]
    others = [
        [on_y(q)(block) for q, block in zip(order, blocks)] for order, blocks in zip(orders, sent)
    ]
    totals = [
        reduced_on_y(pairs[0], after(others[0], sent[1])),
        reduced_on_y(pairs[1], others[1]),
    ]
    sent = [total.astype(BF16) for total in totals]
    others = [on_z_hi(total) for total in sent]
    first = local(totals[0], after(others[0], sent[1]))
    second = local(totals[1], others[1])
    others = [
        after([on_y(q)(first) for q in (1, 2, 3)], second),
        after([on_y(q)(second) for q in (3, 2, 1)], first)[::-1],
    ]
    halves = [jnp.concatenate([a] + b, axis=1) for a, b in zip((first, second), others)]
    others = [on_core(half) for half in halves]
    fulls = [joined(halves[0], others[0])]
    back = input_part(fulls[0])
    back, sent = back[:64], back[64:]
    fulls.append(joined(halves[1], after(others[1], sent)))
    passed = on_x(1)(sent)
    last = input_part(fulls[1])
    back_total = back + on_x(3)(last[64:] + passed) + on_x(1)(last[:64])
    back_total = xor_blocks(back_total, place)
    total = back_total[:16]
    for k in (1, 2, 3):
        total = total + on_z_lo(k)(back_total[16 * k : 16 * k + 16])
    input_grad = total.astype(BF16)

    panel = jnp.concatenate((own, rest), axis=0)
    cots = jnp.concatenate(after(fulls, last), axis=0)
    factor = F32(panel.shape[0]) ** (-0.5)
    token, cot = panel[:, :depth], panel[:, depth:]
    rows = ((0,), (0,))
    down_grad = (dot(cots[:, :width], cot, rows) * factor).astype(BF16)
    gate_grad = (dot(token, cots[:, width : 2 * width], rows) * factor).astype(BF16)
    up_grad = (dot(token, cots[:, 2 * width :], rows) * factor).astype(BF16)
    return (input_grad, gate_grad, up_grad, down_grad)


def solution(mesh):
    in_specs = (P("row", "col"), P("col", "row"), P("col", "row"), P("row", "col"), P("row", "col"))
    out_specs = (P("row", "col"), P("col", "row"), P("col", "row"), P("row", "col"))
    return jax.shard_map(body, mesh=mesh, in_specs=in_specs, out_specs=out_specs, check_vma=False)
```

```python
import jax
import jax.numpy as jnp
from jax import lax
from jax.sharding import PartitionSpec as P

F32 = jnp.float32
BF16 = jnp.bfloat16


def swapped(axis, mask):
    return lambda a: lax.ppermute(a, axis, [(i, i ^ mask) for i in range(16)])


def on_x(k):
    return swapped("row", k)


def on_z_lo(k):
    return swapped("row", 4 * k)


def on_y(k):
    return swapped("col", 4 * k)


on_z_hi = swapped("col", 2)
on_core = swapped("col", 1)

def xor_blocks(a, place):
    for bit, size in ((4, 32), (2, 16), (1, 8)):
        parts = a.reshape(-1, 2, size, a.shape[1])
        other = jnp.stack((parts[:, 1], parts[:, 0]), axis=1)
        a = jnp.where((place & bit) > 0, other, parts).reshape(a.shape)
    return a


def pointwise(gate, up, hidden_cot):
    sigma = jax.nn.sigmoid(gate)
    silu = gate * sigma
    hidden = (silu * up).astype(BF16)
    up_cot = (hidden_cot * silu).astype(BF16)
    gate_cot = (hidden_cot * up * sigma * (1.0 + gate * (1.0 - sigma))).astype(BF16)
    return jnp.concatenate((hidden, gate_cot, up_cot), axis=-1)


def dot(left, right, dims):
    return lax.dot_general(left, right, (dims, ((), ())), preferred_element_type=F32)


def side_by_side(left, right):
    n = left.shape[1]
    zero = jnp.zeros((), left.dtype)
    return lax.pad(left, zero, ((0, 0, 0), (0, n, 0))) + lax.pad(right, zero, ((0, 0, 0), (n, 0, 0)))


def after(value, other):
    return lax.optimization_barrier((value, other))[0]


def in_order(values, order):
    return [values[order.index(k)] for k in (1, 2, 3)]


def body(tokens, gate_weight, up_weight, down_weight, out_grad):
    width = gate_weight.shape[1]
    depth = tokens.shape[1]
    col = lax.axis_index("col")
    place = (col % 2) * 4 + col // 4

    both = side_by_side(tokens, out_grad)
    own = jnp.concatenate([both] + [on_z_lo(k)(both) for k in (1, 2, 3)], axis=0)
    own = xor_blocks(own, place)
    near, far = on_x(2)(own), [on_x(1)(own), on_x(3)(own)]

    def partial_sums(chunk):
        token, cot = chunk[:, :depth], chunk[:, depth:]
        return jnp.concatenate(
            (
                dot(token, gate_weight, ((1,), (0,))),
                dot(token, up_weight, ((1,), (0,))),
                dot(cot, down_weight, ((1,), (1,))),
            ),
            axis=1,
        ).reshape(-1, 64, 3 * width)

    def reduced_on_core(part):
        return part[:, :32] + on_core(part[:, 32:])

    def sent_on_y(pair, order):
        return [pair[:, 8 * q : 8 * q + 8].astype(BF16) for q in order]

    def reduced_on_y(pair, others):
        total = pair[:, :8]
        for other in others:
            total = total + other.astype(F32)
        return total

    def local(total, other):
        total = total + other.astype(F32)
        return pointwise(total[..., :width], total[..., width : 2 * width], total[..., 2 * width :])

    def joined(half, other):
        return jnp.concatenate((half, other), axis=1).reshape(128, 3 * width)

    def input_part(full):
        return dot(full[:, width : 2 * width], gate_weight, ((1,), (1,))) + dot(
            full[:, 2 * width :], up_weight, ((1,), (1,))
        )

    part = partial_sums(own)
    pair = reduced_on_core(part)
    rest = jnp.concatenate(after(far + [near], part), axis=0)
    part = partial_sums(rest)
    pairs = [
        jnp.concatenate((pair, reduced_on_core(part[2:])), axis=0),
        reduced_on_core(part[:2]),
    ]
    orders = ((1, 2, 3), (3, 1, 2))
    sent = [sent_on_y(pair, order) for pair, order in zip(pairs, orders)]
    others = [
        [on_y(q)(block) for q, block in zip(order, blocks)] for order, blocks in zip(orders, sent)
    ]
    totals = [
        reduced_on_y(pairs[0], after(others[0], sent[1])),
        reduced_on_y(pairs[1], others[1]),
    ]
    sent = [total.astype(BF16) for total in totals]
    others = [on_z_hi(total) for total in sent]
    first = local(totals[0], after(others[0], sent[1]))
    second = local(totals[1], others[1])
    others = [
        in_order(after([on_y(q)(first) for q in (2, 1, 3)], second), (2, 1, 3)),
        in_order(after([on_y(q)(second) for q in (2, 1, 3)], first), (2, 1, 3)),
    ]
    halves = [jnp.concatenate([a] + b, axis=1) for a, b in zip((first, second), others)]
    others = [on_core(half) for half in halves]
    fulls = [joined(halves[0], others[0])]
    back = input_part(fulls[0])
    back, sent = back[:64], back[64:]
    fulls.append(joined(halves[1], after(others[1], sent)))
    back_total = back + on_x(2)(sent)
    back = input_part(fulls[1])
    back_total = back_total + on_x(3)(back[64:]) + on_x(1)(back[:64])
    back_total = xor_blocks(back_total, place)
    total = back_total[:16]
    for k in (3, 1, 2):
        total = total + on_z_lo(k)(back_total[16 * k : 16 * k + 16])
    input_grad = total.astype(BF16)

    panel = jnp.concatenate((own, near, rest[:128]), axis=0)
    cots = after(jnp.concatenate(fulls, axis=0), back)
    factor = F32(panel.shape[0]) ** (-0.5)
    token, cot = panel[:, :depth], panel[:, depth:]
    rows = ((0,), (0,))
    down_grad = (dot(cots[:, :width], cot, rows) * factor).astype(BF16)
    gate_grad = (dot(token, cots[:, width : 2 * width], rows) * factor).astype(BF16)
    up_grad = (dot(token, cots[:, 2 * width :], rows) * factor).astype(BF16)
    return (input_grad, gate_grad, up_grad, down_grad)


def solution(mesh):
    in_specs = (P("row", "col"), P("col", "row"), P("col", "row"), P("row", "col"), P("row", "col"))
    out_specs = (P("row", "col"), P("col", "row"), P("col", "row"), P("row", "col"))
    return jax.shard_map(body, mesh=mesh, in_specs=in_specs, out_specs=out_specs, check_vma=False)
```

```python
import jax
import jax.numpy as jnp
from jax import lax
from jax.sharding import PartitionSpec as P

F32 = jnp.float32
BF16 = jnp.bfloat16


def swapped(axis, mask):
    return lambda a: lax.ppermute(a, axis, [(i, i ^ mask) for i in range(16)])


def on_x(k):
    return swapped("row", k)


def on_z_lo(k):
    return swapped("row", 4 * k)


def on_y(k):
    return swapped("col", 4 * k)


on_z_hi = swapped("col", 2)
on_core = swapped("col", 1)

def xor_blocks(a, place):
    for bit, size in ((4, 32), (2, 16), (1, 8)):
        parts = a.reshape(-1, 2, size, a.shape[1])
        other = jnp.stack((parts[:, 1], parts[:, 0]), axis=1)
        a = jnp.where((place & bit) > 0, other, parts).reshape(a.shape)
    return a


def pointwise(gate, up, hidden_cot):
    sigma = jax.nn.sigmoid(gate)
    silu = gate * sigma
    hidden = (silu * up).astype(BF16)
    up_cot = (hidden_cot * silu).astype(BF16)
    gate_cot = (hidden_cot * up * sigma * (1.0 + gate * (1.0 - sigma))).astype(BF16)
    return jnp.concatenate((hidden, gate_cot, up_cot), axis=-1)


def dot(left, right, dims):
    return lax.dot_general(left, right, (dims, ((), ())), preferred_element_type=F32)


def side_by_side(left, right):
    n = left.shape[1]
    zero = jnp.zeros((), left.dtype)
    return lax.pad(left, zero, ((0, 0, 0), (0, n, 0))) + lax.pad(right, zero, ((0, 0, 0), (n, 0, 0)))


def after(value, other):
    return lax.optimization_barrier((value, other))[0]


def in_order(values, order):
    return [values[order.index(k)] for k in (1, 2, 3)]


def body(tokens, gate_weight, up_weight, down_weight, out_grad):
    width = gate_weight.shape[1]
    depth = tokens.shape[1]
    col = lax.axis_index("col")
    place = (col % 2) * 4 + col // 4

    both = side_by_side(tokens, out_grad)
    own = jnp.concatenate([both] + [on_z_lo(k)(both) for k in (1, 2, 3)], axis=0)
    own = xor_blocks(own, place)
    near, far = on_x(2)(own), [on_x(1)(own), on_x(3)(own)]

    def partial_sums(chunk):
        token, cot = chunk[:, :depth], chunk[:, depth:]
        return jnp.concatenate(
            (
                dot(token, gate_weight, ((1,), (0,))),
                dot(token, up_weight, ((1,), (0,))),
                dot(cot, down_weight, ((1,), (1,))),
            ),
            axis=1,
        ).reshape(-1, 64, 3 * width)

    def reduced_on_core(part):
        return part[:, :32] + on_core(part[:, 32:])

    def sent_on_y(pair, order):
        return [pair[:, 8 * q : 8 * q + 8].astype(BF16) for q in order]

    def reduced_on_y(pair, others):
        total = pair[:, :8]
        for other in others:
            total = total + other.astype(F32)
        return total

    def local(total, other):
        total = total + other.astype(F32)
        return pointwise(total[..., :width], total[..., width : 2 * width], total[..., 2 * width :])

    def joined(half, other):
        return jnp.concatenate((half, other), axis=1).reshape(128, 3 * width)

    def input_part(full):
        return dot(full[:, width : 2 * width], gate_weight, ((1,), (1,))) + dot(
            full[:, 2 * width :], up_weight, ((1,), (1,))
        )

    part = partial_sums(own)
    pair = reduced_on_core(part)
    rest = jnp.concatenate(after(far + [near], part), axis=0)
    part = partial_sums(rest)
    pairs = [
        jnp.concatenate((pair, reduced_on_core(part[2:])), axis=0),
        reduced_on_core(part[:2]),
    ]
    orders = ((1, 2, 3), (3, 1, 2))
    sent = [sent_on_y(pair, order) for pair, order in zip(pairs, orders)]
    others = [
        [on_y(q)(block) for q, block in zip(order, blocks)] for order, blocks in zip(orders, sent)
    ]
    totals = [
        reduced_on_y(pairs[0], after(others[0], sent[1])),
        reduced_on_y(pairs[1], others[1]),
    ]
    sent = [total.astype(BF16) for total in totals]
    others = [on_z_hi(total) for total in sent]
    first = local(totals[0], after(others[0], sent[1]))
    second = local(totals[1], others[1])
    others = [
        in_order(after([on_y(q)(first) for q in (2, 1, 3)], second), (2, 1, 3)),
        in_order(after([on_y(q)(second) for q in (2, 1, 3)], first), (2, 1, 3)),
    ]
    halves = [jnp.concatenate([a] + b, axis=1) for a, b in zip((first, second), others)]
    others = [on_core(half) for half in halves]
    fulls = [joined(halves[0], others[0])]
    back = input_part(fulls[0])
    back, sent = back[:64], back[64:]
    fulls.append(joined(halves[1], after(others[1], sent)))
    back_total = back + on_x(2)(sent)
    back = input_part(fulls[1])
    back_total = back_total + on_x(3)(back[64:]) + on_x(1)(back[:64])
    back_total = xor_blocks(back_total, place)
    total = back_total[:16]
    for k in (3, 1, 2):
        total = total + on_z_lo(k)(back_total[16 * k : 16 * k + 16])
    input_grad = total.astype(BF16)

    panel = jnp.concatenate((own, near, rest[:128]), axis=0)
    cots = jnp.concatenate(after(fulls, back), axis=0)
    factor = F32(panel.shape[0]) ** (-0.5)
    token, cot = panel[:, :depth], panel[:, depth:]
    rows = ((0,), (0,))
    down_grad = (dot(cots[:, :width], cot, rows) * factor).astype(BF16)
    gate_grad = (dot(token, cots[:, width : 2 * width], rows) * factor).astype(BF16)
    up_grad = (dot(token, cots[:, 2 * width :], rows) * factor).astype(BF16)
    return (input_grad, gate_grad, up_grad, down_grad)


def solution(mesh):
    in_specs = (P("row", "col"), P("col", "row"), P("col", "row"), P("row", "col"), P("row", "col"))
    out_specs = (P("row", "col"), P("col", "row"), P("col", "row"), P("row", "col"))
    return jax.shard_map(body, mesh=mesh, in_specs=in_specs, out_specs=out_specs, check_vma=False)
```
